32 devices in a mesh: clip: 2 (over x), tile: 16 (over z, y, core).
Axes of the slice: x: 2, y: 2, z: 4, core: 2. Of those that a mesh axis runs over, the one named last changes fastest.
Arguments:
- queries: bfloat16 [128, 256, 256], P(('clip', 'tile')), parts along dimension 0, may hold values from -150 to 150
- keys: bfloat16 [128, 256, 256], P(('clip', 'tile')), parts along dimension 0, may hold values from -7 to 7
- values: bfloat16 [128, 256, 256], P(('clip', 'tile')), parts along dimension 0, may hold values from -6 to 6
- counts: int32 [32], P('clip'), parts along dimension 0, may hold values from 3 to 4, as said below
- neighbors: int32 [112, 45], P('clip'), parts along dimension 0, may hold values from -1 to 55, as said below
Outputs:
- attended: bfloat16 [128, 256, 256], P(('clip', 'tile')), parts along dimension 0
The draws below stay inside these ranges and needn't reach their ends.
There are 2 independent parts, one for each index of `clip`. The reference program is written for one: setup_inputs(seed, part) draws one part's arguments, and reference() takes and returns one part's arrays. A program takes and returns all parts, laid end to end along the dimension named above; each array names one. Nothing has to cross between parts.
Inputs may be any that keep to these rules, and one draw needn't show every extreme that they name: `counts`: entries sum to 56; some device owns exactly 4 tiles and some exactly 3. `neighbors`: row t lists 3 x 3 x 5 tiles: the slabs from t's slab - 1 to + 1 and the rows from t's row - 1 to + 1 (-1 where these lie outside the grid), and 5 consecutive columns inside the grid that contain t's column. So every listed id lies within 39 of t, and t lists itself.
All inputs are finite; a program needn't handle non-finite values.
Results may differ from the reference program's by a relative error of at most 0.0033.
Values may be sent and summed in bfloat16 or wider, within the bound.
A program may use at most 128 MiB of HBM per device.

```python
import jax
import jax.numpy as jnp
from jax import lax

HEADS = 2
HD = 128
TOK = 256
GH = 4
GW = 7
NBR = 45
PAIR = 7
TILES = 56
GT = 2
LEAST = 3
MOST = 4
SLOTS = 64
N_TILE = 16


def draw_keys(key, part):
    key = jax.random.fold_in(key, 3)
    return jnp.clip(jax.random.normal(key, (SLOTS, TOK, HEADS * HD), jnp.float32), -6.0, 6.0).astype(jnp.bfloat16)


def draw_queries(key, part):
    key = jax.random.fold_in(key, 4)
    return jnp.clip(2.5 * jax.random.normal(key, (SLOTS, TOK, HEADS * HD), jnp.float32), -15.0, 15.0).astype(jnp.bfloat16)


def draw_counts(key, part):
    key = jax.random.fold_in(key, 5)
    first_key, second_key = jax.random.split(key)
    halves = N_TILE // 2
    first = jax.random.randint(first_key, (halves,), LEAST, MOST + 1, jnp.int32)
    first = first.at[0].set(MOST)
    second = PAIR - first
    paired = jnp.stack([first, second], axis=1).reshape(N_TILE)
    order = jax.random.permutation(second_key, N_TILE)
    return paired[order].astype(jnp.int32)


def draw_neighbors(key, part):
    key = jax.random.fold_in(key, 7)
    tile_ids = jnp.arange(TILES, dtype=jnp.int32)
    slab_size = GH * GW
    frame = tile_ids // slab_size
    within = tile_ids % slab_size
    row_index = within // GW
    column = within % GW
    lowest = jnp.maximum(column - 4, 0)
    highest = jnp.minimum(column, GW - 5)
    raw_pick = jax.random.randint(key, (TILES,), 0, 1 << 20, jnp.int32)
    first_column = lowest + raw_pick % (highest - lowest + 1)
    steps_three = jnp.arange(3, dtype=jnp.int32) - 1
    steps_five = jnp.arange(5, dtype=jnp.int32)
    frames = frame[:, None, None, None] + steps_three[None, :, None, None]
    rows_all = row_index[:, None, None, None] + steps_three[None, None, :, None]
    columns = first_column[:, None, None, None] + steps_five[None, None, None, :]
    inside = (frames >= 0) & (frames < GT) & (rows_all >= 0) & (rows_all < GH)
    listed = jnp.where(inside, (frames * GH + rows_all) * GW + columns, -1)
    return listed.reshape(TILES, 45).astype(jnp.int32)


def steps_of(key, shape, cuts, smallest, top_value):
    level = 1.0
    for axis_at, blocks in cuts:
        steps = jax.random.uniform(jax.random.fold_in(jax.random.fold_in(key, 6), axis_at), (blocks,), jnp.float32, smallest / len(cuts), top_value / len(cuts))
        level = level * jnp.repeat(jnp.exp(steps), shape[axis_at] // blocks).reshape((-1,) + (1,) * (len(shape) - 1 - axis_at))
    return level


def centred(own_key, shape, spread, reach, cuts=(), kind=jnp.bfloat16):
    entries = spread * jax.random.normal(own_key, shape, jnp.float32)
    if cuts:
        entries = entries * steps_of(own_key, shape, cuts, -0.22, 0.18)
    return jnp.clip(entries, -reach, reach).astype(kind)


def setup_inputs(seed: int = 0, part: int = 0) -> dict:
    splits = jax.random.split(jax.random.key(seed), 6)
    own_keys = jax.random.split(jax.random.fold_in(splits[5], part), 6)
    queries = draw_queries(jax.random.fold_in(jax.random.fold_in(splits[5], part), 71), part)
    keys = draw_keys(jax.random.fold_in(jax.random.fold_in(splits[5], part), 71), part)
    values = centred(own_keys[2], (SLOTS, TOK, HEADS * HD), 1.0, 6.0, ((0, 16),))
    counts = draw_counts(jax.random.fold_in(jax.random.fold_in(splits[5], part), 71), part)
    neighbors = draw_neighbors(jax.random.fold_in(jax.random.fold_in(splits[5], part), 71), part)
    return {"queries": queries, "keys": keys, "values": values, "counts": counts, "neighbors": neighbors}


masked_score = -1e30


def attend_tile(query_tile, key_tiles, value_tiles, usable):
    query_full = query_tile.astype(jnp.float32).reshape(TOK, HEADS, HD)
    key_full = key_tiles.astype(jnp.float32).reshape(NBR * TOK, HEADS, HD)
    value_full = value_tiles.astype(jnp.float32).reshape(NBR * TOK, HEADS, HD)
    scores = jnp.einsum("qhd,khd->hqk", query_full, key_full) * (HD ** -0.5)
    keep_keys = jnp.repeat(usable, TOK, total_repeat_length=NBR * TOK)
    scores = jnp.where(keep_keys[None, None, :], scores, masked_score)
    highest = jnp.max(scores, axis=-1, keepdims=True)
    weights = jnp.exp(scores - highest)
    totals = jnp.sum(weights, axis=-1)
    probs = weights.astype(jnp.bfloat16).astype(jnp.float32)
    mixed = jnp.einsum("hqk,khd->qhd", probs, value_full)
    mixed = mixed / jnp.transpose(totals)[:, :, None]
    return mixed.astype(jnp.bfloat16).reshape(TOK, HEADS * HD)


def reference(queries, keys, values, counts, neighbors):
    owned = counts.astype(jnp.int32)
    ends = jnp.cumsum(owned).astype(jnp.int32)
    starts = (ends - owned).astype(jnp.int32)
    tile_ids = jnp.arange(TILES, dtype=jnp.int32)
    owner = (jnp.sum((starts[None, :] <= tile_ids[:, None]).astype(jnp.int32), axis=1) - 1).astype(jnp.int32)
    slot_rows = (owner * MOST + tile_ids - starts[owner]).astype(jnp.int32)
    query_all = queries[slot_rows]
    key_all = keys[slot_rows]
    value_all = values[slot_rows]

    def per_tile(tile_id):
        listed = neighbors[tile_id]
        usable = listed >= 0
        safe_ids = jnp.clip(listed, 0, TILES - 1).astype(jnp.int32)
        return attend_tile(query_all[tile_id], key_all[safe_ids], value_all[safe_ids], usable)

    attended_all = lax.map(per_tile, tile_ids)
    slot_ids = jnp.arange(SLOTS, dtype=jnp.int32)
    device = (slot_ids // MOST).astype(jnp.int32)
    within = (slot_ids % MOST).astype(jnp.int32)
    used = within < owned[device]
    source = jnp.clip(starts[device] + within, 0, TILES - 1).astype(jnp.int32)
    return jnp.where(used[:, None, None], attended_all[source], jnp.zeros((), jnp.bfloat16))
```

```python
import math

import jax
import jax.numpy as jnp
from jax import lax
from jax.experimental import pallas as pl
from jax.experimental.pallas import tpu as pltpu
from jax.sharding import PartitionSpec as P

HEADS = 2
NBR = 45
REACH = 13


masked_score = -1e30


def passed_along(value, axis, steps):
    count = lax.axis_size(axis)
    initial, last = (max(0, -steps), min(count, count - steps))
    return lax.ppermute(value, axis, [(source, source + steps) for source in range(initial, last)])


def ring_attention(queries, keys, values, counts, neighbors):
    capacity = queries.shape[0]
    tokens = queries.shape[1]
    channels = queries.shape[2]
    head_dim = channels // HEADS
    device_count = counts.shape[0]
    position = lax.axis_index("tile")
    ends = jnp.cumsum(counts)
    starts = ends - counts
    owned = counts[position]
    first_id = starts[position]
    paired = jnp.concatenate([keys, values], axis=2)
    earlier = []
    later = []
    carried_before = paired
    carried_after = paired
    for step in range(REACH):
        carried_before = passed_along(carried_before, "tile", 1)
        carried_after = passed_along(carried_after, "tile", -1)
        earlier.append(carried_before)
        later.append(carried_after)
    window = jnp.concatenate(earlier[::-1] + [paired] + later, axis=0)
    window_size = window.shape[0]
    factor = head_dim ** (-0.5)

    def attend(offset, output):
        tile_id = first_id + offset
        listed = lax.dynamic_index_in_dim(neighbors, tile_id, 0, keepdims=False)
        usable = listed >= 0
        owner_of = jnp.sum((starts[None, :] <= listed[:, None]).astype(jnp.int32), axis=1) - 1
        owner_of = jnp.clip(owner_of, 0, device_count - 1)
        places = (owner_of - position + REACH) * capacity + listed - starts[owner_of]
        places = jnp.clip(places, 0, window_size - 1)
        picked = jnp.take(window, places, axis=0)
        query_tile = lax.dynamic_index_in_dim(queries, offset, 0, keepdims=False)
        keep_keys = jnp.repeat(usable, tokens, total_repeat_length=NBR * tokens)
        results = []
        for head in range(HEADS):
            low = head * head_dim
            key_block = picked[:, :, low : low + head_dim].reshape(NBR * tokens, head_dim)
            value_block = picked[:, :, channels + low : channels + low + head_dim].reshape(
                NBR * tokens, head_dim
            )
            query_head = query_tile[:, low : low + head_dim]
            scores = (
                lax.dot_general(
                    query_head,
                    key_block,
                    (((1,), (1,)), ((), ())),
                    preferred_element_type=jnp.float32,
                )
                * factor
            )
            scores = jnp.where(keep_keys[None, :], scores, masked_score)
            highest = jnp.max(scores, axis=-1, keepdims=True)
            weights = jnp.exp(scores - highest)
            totals = jnp.sum(weights, axis=-1)
            probs = weights.astype(jnp.bfloat16)
            mixed = jnp.dot(probs, value_block, preferred_element_type=jnp.float32)
            mixed = mixed / totals[:, None]
            results.append(mixed.astype(jnp.bfloat16))
        result = jnp.concatenate(results, axis=1)
        return lax.dynamic_update_index_in_dim(output, result, offset, 0)

    blank = jnp.zeros_like(queries)
    return lax.fori_loop(0, owned, attend, blank)


LINE = 4
CORES = 2
LISTED_OUT = 3e30
NOTHING_YET = -1e30
AHEAD = 1


def gathered_kernel(aside_ref, q_ref, k_ref, v_ref, o_ref, kv, top, total, acc,
                    arrive, to_sib, to_a, to_b, to_c):
    capacity, tokens, channels = q_ref.shape
    head_dim = channels // HEADS
    scale = math.log2(math.e) / math.sqrt(head_dim)
    me = lax.axis_index("tile")
    core = me % 2
    y = (me // 2) % 2
    z = me // 4
    side = z // 2
    outer = (z == 0) | (z == LINE - 1)
    inner = jnp.logical_not(outer)
    z_o, z_i, z_m, z_f = 3 * side, 1 + side, 2 - side, 3 - 3 * side
    flip = 1 - 2 * core

    def at(zz, yy):
        return (zz * 2 + yy) * 2 + core

    sibling = me + flip
    across = at(z, 1 - y)
    near = at(jnp.where(outer, z_i, z_o), y)
    middle = at(z_m, y)

    def send(g, sem, target):
        return pltpu.make_async_remote_copy(
            src_ref=kv.at[g], dst_ref=kv.at[g], send_sem=sem, recv_sem=arrive.at[g],
            device_id={"tile": target}, device_id_type=pl.DeviceIdType.MESH)

    def landed(g):
        send(g, to_sib.at[0], sibling).wait_recv()

    def outer_slot(m):
        k = m // 2
        first = m % 2 == 0
        along = jnp.where(k < 4, at(z_i, y) * 4 + k, jnp.where(k < 8, at(z_m, y) * 4 + k - 4, jnp.where(
            k < 12, at(z_f, y) * 4 + k - 8, at(z_i, 1 - y) * 4 + k - 12)))
        over = jnp.where(k < 4, at(z_o, 1 - y) * 4 + k, jnp.where(k < 6, at(z_i, 1 - y) * 4 + k - 2, jnp.where(
            k < 10, at(z_m, 1 - y) * 4 + k - 6, at(z_f, 1 - y) * 4 + k - 10)))
        return jnp.where(first, along, over)

    def inner_slot(m):
        k = (m // 3) % 4
        lane = m % 3
        one = jnp.where(lane == 0, at(z_o, y), jnp.where(lane == 1, at(z_m, y), at(z_i, 1 - y)))
        two = jnp.where(lane == 0, at(z_o, 1 - y), jnp.where(lane == 1, at(z_f, y), at(z_f, 1 - y)))
        return jnp.where(m < 12, one * 4 + k, jnp.where(m < 24, two * 4 + k, at(z_m, 1 - y) * 4 + m - 24))

    def slot_of(j):
        m = jnp.maximum(j - 4, 0)
        later = jnp.where(outer, outer_slot(m), inner_slot(m))
        return jnp.where(j < 4, me * 4 + j, later)

    barrier = pltpu.get_barrier_semaphore()
    for other in (sibling, across, near):
        pl.semaphore_signal(barrier, inc=1, device_id={"tile": other}, device_id_type=pl.DeviceIdType.MESH)

    @pl.when(inner)
    def _():
        pl.semaphore_signal(barrier, inc=1, device_id={"tile": middle}, device_id_type=pl.DeviceIdType.MESH)
        pl.semaphore_wait(barrier, 4)

    @pl.when(outer)
    def _():
        pl.semaphore_wait(barrier, 3)

    for s in range(capacity):
        g = me * 4 + s
        kv[g, 0] = k_ref[s]
        kv[g, 1] = v_ref[s].T
        send(g, to_a.at[s], near).start()
        send(g, to_b.at[s], across).start()
        send(g, to_sib.at[s], sibling).start()

        @pl.when(inner)
        def _():
            send(g, to_c.at[s], middle).start()

    top[...] = jnp.full(top.shape, NOTHING_YET, jnp.float32)
    total[...] = jnp.zeros(total.shape, jnp.float32)
    acc[...] = jnp.zeros(acc.shape, jnp.float32)

    def pass_on(j):
        g = slot_of(j)
        m = j - 4
        landed(g)

        @pl.when(outer)
        def _():
            k = m // 2
            along = m % 2 == 0

            @pl.when(along & (k >= 2) & (k < 12))
            def _():
                send(g, to_b.at[k + 2], across).start()

            @pl.when(jnp.logical_not(along) & (k < 4))
            def _():
                send(g, to_a.at[k + 4], near).start()

        @pl.when(inner & (m < 24))
        def _():
            k = (m // 3) % 4
            lane = m % 3
            early = m < 12
            kept = at(z_i, 1 - y) * 4

            @pl.when(lane == 0)
            def _():
                send(jnp.where(early, g, kept + k), to_c.at[jnp.where(early, 4, 8) + k], middle).start()

            @pl.when(lane == 1)
            def _():
                send(g, to_a.at[jnp.where(early, 4, 8) + k], near).start()

                @pl.when(jnp.logical_not(early))
                def _():
                    send(g, to_b.at[4 + k], across).start()

                    @pl.when(k >= 2)
                    def _():
                        send(kept + k - 2, to_a.at[10 + k], near).start()

        send(g, to_sib.at[j], sibling).start()

    def attend(first, second):
        for head in range(HEADS):
            low = head * head_dim
            keys = [kv[g, 0, :, low : low + head_dim] for g in (first, second)]
            values = [kv[g, 1, low : low + head_dim, :] for g in (first, second)]
            for r in range(capacity):
                unit = r * HEADS + head
                query = q_ref[r, :, low : low + head_dim]
                aside = [aside_ref[r, g] for g in (first, second)]
                scores = [
                    lax.dot_general(key, query, (((1,), (1,)), ((), ())), preferred_element_type=jnp.float32)
                    for key in keys
                ]
                before = top[unit]
                now = before
                for score, off in zip(scores, aside):
                    now = jnp.maximum(now, jnp.max(score, axis=0, keepdims=True) * scale - off)
                fade = jnp.exp2(before - now)
                summed = total[unit] * fade
                mixed = acc[unit] * fade
                for score, off, value in zip(scores, aside, values):
                    weights = jnp.exp2(score * scale - (now + off))
                    summed += jnp.sum(weights, axis=0, keepdims=True)
                    mixed += jnp.dot(value, weights.astype(jnp.bfloat16), preferred_element_type=jnp.float32)
                top[unit] = now
                total[unit] = summed
                acc[unit] = mixed

    steps = 32

    def step(j, _):
        @pl.when((j + AHEAD >= 4) & (j + AHEAD < steps))
        def _():
            pass_on(j + AHEAD)

        mine = slot_of(j)
        theirs = mine + 4 * flip
        landed(theirs)
        attend(mine, theirs)
        return 0

    lax.fori_loop(0, steps, step, 0)

    for r in range(capacity):
        for head in range(HEADS):
            unit = r * HEADS + head
            low = head * head_dim
            sums = total[unit]
            share = jnp.where(sums > 0, 1.0 / sums, 0.0)
            o_ref[r, :, low : low + head_dim] = (acc[unit] * share).T.astype(o_ref.dtype)

    def sent(sems, target, count):
        def one(n, _):
            send(me * 4, sems.at[n], target).wait_send()
            return 0

        lax.fori_loop(0, count, one, 0)

    sent(to_sib, sibling, steps)

    @pl.when(outer)
    def _():
        sent(to_a, near, 8)
        sent(to_b, across, 14)

    @pl.when(inner)
    def _():
        sent(to_a, near, 14)
        sent(to_b, across, 8)
        sent(to_c, middle, 12)


def gathered_attention(queries, keys, values, counts, neighbors):
    capacity, tokens, channels = queries.shape
    device_count = counts.shape[0]
    slots = device_count * capacity
    head_dim = channels // HEADS
    position = lax.axis_index("tile")
    ids = jnp.arange(device_count)
    starts = jnp.sum(jnp.where(ids[None, :] < ids[:, None], counts[None, :], 0), axis=1)
    within = jnp.arange(capacity)
    held = jnp.where(within[None, :] < counts[:, None], starts[:, None] + within[None, :], -2).reshape(slots)
    first = jnp.sum(jnp.where(ids < position, counts, 0))
    owned = jnp.sum(jnp.where(ids == position, counts, 0))
    rows = jnp.minimum(first + within, neighbors.shape[0] - 1)
    listed = jnp.take(neighbors, rows, axis=0)
    wanted = jnp.any(listed[:, :, None] == held[None, None, :], axis=1) & (within < owned)[:, None]
    aside = jnp.where(wanted, 0.0, LISTED_OUT).astype(jnp.float32)
    units = capacity * HEADS
    return pl.pallas_call(
        gathered_kernel,
        out_shape=jax.ShapeDtypeStruct(queries.shape, queries.dtype),
        in_specs=[pl.BlockSpec(memory_space=pltpu.SMEM)] + [pl.BlockSpec(memory_space=pltpu.VMEM)] * 3,
        out_specs=pl.BlockSpec(memory_space=pltpu.VMEM),
        scratch_shapes=[
            pltpu.VMEM((slots, 2, tokens, channels), keys.dtype),
            pltpu.VMEM((units, 1, tokens), jnp.float32),
            pltpu.VMEM((units, 1, tokens), jnp.float32),
            pltpu.VMEM((units, head_dim, tokens), jnp.float32),
            pltpu.SemaphoreType.DMA((slots,)),
            pltpu.SemaphoreType.DMA((32,)),
            pltpu.SemaphoreType.DMA((14,)),
            pltpu.SemaphoreType.DMA((14,)),
            pltpu.SemaphoreType.DMA((12,)),
        ],
        compiler_params=pltpu.CompilerParams(
            collective_id=0, has_side_effects=True, vmem_limit_bytes=48 * 1024 * 1024
        ),
        cost_estimate=pl.CostEstimate(
            flops=4 * capacity * slots * tokens * tokens * channels,
            bytes_accessed=4 * queries.size * 2,
            transcendentals=capacity * slots * HEADS * tokens * tokens,
        ),
        name="gathered_attention",
    )(aside, queries, keys, values)


def per_device(queries, keys, values, counts, neighbors):
    if counts.shape[0] == LINE * 2 * CORES and queries.shape[1] == queries.shape[2] and queries.shape[0] == 4:
        return gathered_attention(queries, keys, values, counts, neighbors)
    return ring_attention(queries, keys, values, counts, neighbors)


def solution(mesh):
    in_specs = (
        P(("clip", "tile"), None, None),
        P(("clip", "tile"), None, None),
        P(("clip", "tile"), None, None),
        P("clip"),
        P("clip", None),
    )
    out_specs = P(("clip", "tile"), None, None)
    return jax.shard_map(
        per_device, mesh=mesh, in_specs=in_specs, out_specs=out_specs, check_vma=False
    )
```

```python
import math

import jax
import jax.numpy as jnp
from jax import lax
from jax.experimental import pallas as pl
from jax.experimental.pallas import tpu as pltpu
from jax.sharding import PartitionSpec as P

HEADS = 2
NBR = 45
REACH = 13


masked_score = -1e30


def passed_along(value, axis, steps):
    count = lax.axis_size(axis)
    initial, last = (max(0, -steps), min(count, count - steps))
    return lax.ppermute(value, axis, [(source, source + steps) for source in range(initial, last)])


def ring_attention(queries, keys, values, counts, neighbors):
    capacity = queries.shape[0]
    tokens = queries.shape[1]
    channels = queries.shape[2]
    head_dim = channels // HEADS
    device_count = counts.shape[0]
    position = lax.axis_index("tile")
    ends = jnp.cumsum(counts)
    starts = ends - counts
    owned = counts[position]
    first_id = starts[position]
    paired = jnp.concatenate([keys, values], axis=2)
    earlier = []
    later = []
    carried_before = paired
    carried_after = paired
    for step in range(REACH):
        carried_before = passed_along(carried_before, "tile", 1)
        carried_after = passed_along(carried_after, "tile", -1)
        earlier.append(carried_before)
        later.append(carried_after)
    window = jnp.concatenate(earlier[::-1] + [paired] + later, axis=0)
    window_size = window.shape[0]
    factor = head_dim ** (-0.5)

    def attend(offset, output):
        tile_id = first_id + offset
        listed = lax.dynamic_index_in_dim(neighbors, tile_id, 0, keepdims=False)
        usable = listed >= 0
        owner_of = jnp.sum((starts[None, :] <= listed[:, None]).astype(jnp.int32), axis=1) - 1
        owner_of = jnp.clip(owner_of, 0, device_count - 1)
        places = (owner_of - position + REACH) * capacity + listed - starts[owner_of]
        places = jnp.clip(places, 0, window_size - 1)
        picked = jnp.take(window, places, axis=0)
        query_tile = lax.dynamic_index_in_dim(queries, offset, 0, keepdims=False)
        keep_keys = jnp.repeat(usable, tokens, total_repeat_length=NBR * tokens)
        results = []
        for head in range(HEADS):
            low = head * head_dim
            key_block = picked[:, :, low : low + head_dim].reshape(NBR * tokens, head_dim)
            value_block = picked[:, :, channels + low : channels + low + head_dim].reshape(
                NBR * tokens, head_dim
            )
            query_head = query_tile[:, low : low + head_dim]
            scores = (
                lax.dot_general(
                    query_head,
                    key_block,
                    (((1,), (1,)), ((), ())),
                    preferred_element_type=jnp.float32,
                )
                * factor
            )
            scores = jnp.where(keep_keys[None, :], scores, masked_score)
            highest = jnp.max(scores, axis=-1, keepdims=True)
            weights = jnp.exp(scores - highest)
            totals = jnp.sum(weights, axis=-1)
            probs = weights.astype(jnp.bfloat16)
            mixed = jnp.dot(probs, value_block, preferred_element_type=jnp.float32)
            mixed = mixed / totals[:, None]
            results.append(mixed.astype(jnp.bfloat16))
        result = jnp.concatenate(results, axis=1)
        return lax.dynamic_update_index_in_dim(output, result, offset, 0)

    blank = jnp.zeros_like(queries)
    return lax.fori_loop(0, owned, attend, blank)


LINE = 4
CORES = 2
LISTED_OUT = 3e30
NOTHING_YET = -1e30
AHEAD = 1


def gathered_kernel(counts_ref, listed_ref, q_ref, k_ref, v_ref, o_ref, kv, values, turned, aside_ref, top,
                    total, acc, own, arrive, to_sib, to_a, to_b, to_c):
    capacity, tokens, channels = q_ref.shape
    head_dim = channels // HEADS
    scale = math.log2(math.e) / math.sqrt(head_dim)
    me = lax.axis_index("tile")
    core = me % 2
    y = (me // 2) % 2
    z = me // 4
    side = z // 2
    outer = (z == 0) | (z == LINE - 1)
    inner = jnp.logical_not(outer)
    z_o, z_i, z_m, z_f = 3 * side, 1 + side, 2 - side, 3 - 3 * side
    flip = 1 - 2 * core

    def at(zz, yy):
        return (zz * 2 + yy) * 2 + core

    sibling = me + flip
    across = at(z, 1 - y)
    near = at(jnp.where(outer, z_i, z_o), y)
    middle = at(z_m, y)

    def send(g, sem, target):
        return pltpu.make_async_remote_copy(
            src_ref=kv.at[g], dst_ref=kv.at[g], send_sem=sem, recv_sem=arrive.at[g],
            device_id={"tile": target}, device_id_type=pl.DeviceIdType.MESH)

    def landed(g):
        send(g, to_sib.at[0], sibling).wait_recv()

    def outer_slot(m):
        k = m // 2
        first = m % 2 == 0
        along = jnp.where(k < 4, at(z_i, y) * 4 + k, jnp.where(k < 8, at(z_m, y) * 4 + k - 4, jnp.where(
            k < 12, at(z_f, y) * 4 + k - 8, at(z_i, 1 - y) * 4 + k - 12)))
        over = jnp.where(k < 4, at(z_o, 1 - y) * 4 + k, jnp.where(k < 6, at(z_i, 1 - y) * 4 + k - 2, jnp.where(
            k < 10, at(z_m, 1 - y) * 4 + k - 6, at(z_f, 1 - y) * 4 + k - 10)))
        return jnp.where(first, along, over)

    def inner_slot(m):
        k = (m // 3) % 4
        lane = m % 3
        one = jnp.where(lane == 0, at(z_o, y), jnp.where(lane == 1, at(z_m, y), at(z_i, 1 - y)))
        two = jnp.where(lane == 0, at(z_o, 1 - y), jnp.where(lane == 1, at(z_f, y), at(z_f, 1 - y)))
        return jnp.where(m < 12, one * 4 + k, jnp.where(m < 24, two * 4 + k, at(z_m, 1 - y) * 4 + m - 24))

    def slot_of(j):
        m = jnp.maximum(j - 4, 0)
        later = jnp.where(outer, outer_slot(m), inner_slot(m))
        return jnp.where(j < 4, me * 4 + j, later)

    staged = [pltpu.make_async_copy(k_ref.at[s], kv.at[me * 4 + s, 0], own.at[s]) for s in range(capacity)]
    staged += [pltpu.make_async_copy(v_ref.at[s], values.at[s], own.at[capacity + s]) for s in range(capacity)]
    staged.append(pltpu.make_async_copy(q_ref, turned, own.at[2 * capacity]))
    for copy in staged:
        copy.start()

    barrier = pltpu.get_barrier_semaphore()
    for other in (sibling, across, near):
        pl.semaphore_signal(barrier, inc=1, device_id={"tile": other}, device_id_type=pl.DeviceIdType.MESH)

    @pl.when(inner)
    def _():
        pl.semaphore_signal(barrier, inc=1, device_id={"tile": middle}, device_id_type=pl.DeviceIdType.MESH)
        pl.semaphore_wait(barrier, 4)

    @pl.when(outer)
    def _():
        pl.semaphore_wait(barrier, 3)

    for s in range(capacity):
        g = me * 4 + s
        staged[s].wait()
        staged[capacity + s].wait()
        kv[g, 1] = values[s].T
        send(g, to_a.at[s], near).start()
        send(g, to_b.at[s], across).start()
        send(g, to_sib.at[s], sibling).start()

        @pl.when(inner)
        def _():
            send(g, to_c.at[s], middle).start()

    staged[2 * capacity].wait()
    for r in range(capacity):
        turned[r] = turned[r].T

    slots = arrive.shape[0]
    device_count = slots // capacity
    shape = (slots, listed_ref.shape[1])
    slot = lax.broadcasted_iota(jnp.int32, shape, 0)
    owner = slot // capacity
    within = slot % capacity
    held = within
    limit = jnp.zeros(shape, jnp.int32)
    first = 0
    owned = 0
    for e in range(device_count):
        held += jnp.where(owner > e, counts_ref[e], 0)
        limit += jnp.where(owner == e, counts_ref[e], 0)
        first += jnp.where(me > e, counts_ref[e], 0)
        owned += jnp.where(me == e, counts_ref[e], 0)
    held = jnp.where(within < limit, held, -2)
    for r in range(capacity):
        row = jnp.minimum(first + r, listed_ref.shape[0] - 1)
        hit = (listed_ref[pl.ds(row, 1), :] == held).astype(jnp.float32)
        wanted = jnp.max(hit, axis=1, keepdims=True) * jnp.where(r < owned, 1.0, 0.0)
        aside_ref[r] = jnp.broadcast_to(jnp.where(wanted > 0, 0.0, LISTED_OUT), (slots, tokens))
    top[...] = jnp.full(top.shape, NOTHING_YET, jnp.float32)
    total[...] = jnp.zeros(total.shape, jnp.float32)
    acc[...] = jnp.zeros(acc.shape, jnp.float32)

    def pass_on(j):
        g = slot_of(j)
        m = j - 4
        landed(g)

        @pl.when(outer)
        def _():
            k = m // 2
            along = m % 2 == 0

            @pl.when(along & (k >= 2) & (k < 12))
            def _():
                send(g, to_b.at[k + 2], across).start()

            @pl.when(jnp.logical_not(along) & (k < 4))
            def _():
                send(g, to_a.at[k + 4], near).start()

        @pl.when(inner & (m < 24))
        def _():
            k = (m // 3) % 4
            lane = m % 3
            early = m < 12
            kept = at(z_i, 1 - y) * 4

            @pl.when(lane == 0)
            def _():
                send(jnp.where(early, g, kept + k), to_c.at[jnp.where(early, 4, 8) + k], middle).start()

            @pl.when(lane == 1)
            def _():
                send(g, to_a.at[jnp.where(early, 4, 8) + k], near).start()

                @pl.when(jnp.logical_not(early))
                def _():
                    send(g, to_b.at[4 + k], across).start()

                    @pl.when(k >= 2)
                    def _():
                        send(kept + k - 2, to_a.at[10 + k], near).start()

        send(g, to_sib.at[j], sibling).start()

    def attend(first, second):
        units = [(r, head) for head in range(HEADS) for r in range(capacity)]

        def scored(n):
            r, head = units[n]
            low = head * head_dim
            return [
                jnp.dot(kv[g, 0, :, low : low + head_dim], turned[r, low : low + head_dim, :],
                        preferred_element_type=jnp.float32)
                for g in (first, second)
            ]

        upcoming = scored(0)
        for n, (r, head) in enumerate(units):
            low = head * head_dim
            unit = r * HEADS + head
            scores = upcoming
            if n + 1 < len(units):
                upcoming = scored(n + 1)
            aside = [aside_ref[r, pl.ds(g, 1), :] for g in (first, second)]
            before = top[unit]
            now = before
            for score, off in zip(scores, aside):
                now = jnp.maximum(now, jnp.max(score, axis=0, keepdims=True) * scale - off)
            fade = jnp.exp2(before - now)
            summed = total[unit] * fade
            mixed = acc[unit] * fade
            for g, score, off in zip((first, second), scores, aside):
                weights = jnp.exp2(score * scale - (now + off))
                summed += jnp.sum(weights, axis=0, keepdims=True)
                mixed += jnp.dot(kv[g, 1, low : low + head_dim, :], weights.astype(jnp.bfloat16),
                                 preferred_element_type=jnp.float32)
            top[unit] = now
            total[unit] = summed
            acc[unit] = mixed

    steps = 32

    def step(j, _):
        @pl.when((j + AHEAD >= 4) & (j + AHEAD < steps))
        def _():
            pass_on(j + AHEAD)

        mine = slot_of(j)
        theirs = mine + 4 * flip
        landed(theirs)
        attend(mine, theirs)
        return 0

    lax.fori_loop(0, steps, step, 0)

    for r in range(capacity):
        for head in range(HEADS):
            unit = r * HEADS + head
            low = head * head_dim
            sums = total[unit]
            share = jnp.where(sums > 0, 1.0 / sums, 0.0)
            o_ref[r, :, low : low + head_dim] = (acc[unit] * share).T.astype(o_ref.dtype)

    def sent(sems, target, count):
        def one(n, _):
            send(me * 4, sems.at[n], target).wait_send()
            return 0

        lax.fori_loop(0, count, one, 0)

    sent(to_sib, sibling, steps)

    @pl.when(outer)
    def _():
        sent(to_a, near, 8)
        sent(to_b, across, 14)

    @pl.when(inner)
    def _():
        sent(to_a, near, 14)
        sent(to_b, across, 8)
        sent(to_c, middle, 12)


def gathered_attention(queries, keys, values, counts, neighbors):
    capacity, tokens, channels = queries.shape
    device_count = counts.shape[0]
    slots = device_count * capacity
    head_dim = channels // HEADS
    units = capacity * HEADS
    return pl.pallas_call(
        gathered_kernel,
        out_shape=jax.ShapeDtypeStruct(queries.shape, queries.dtype),
        in_specs=[pl.BlockSpec(memory_space=pltpu.SMEM), pl.BlockSpec(memory_space=pltpu.VMEM)]
        + [pl.BlockSpec(memory_space=pltpu.HBM)] * 3,
        out_specs=pl.BlockSpec(memory_space=pltpu.VMEM),
        scratch_shapes=[
            pltpu.VMEM((slots, 2, tokens, channels), keys.dtype),
            pltpu.VMEM((capacity, tokens, channels), values.dtype),
            pltpu.VMEM((capacity, channels, tokens), queries.dtype),
            pltpu.VMEM((capacity, slots, tokens), jnp.float32),
            pltpu.VMEM((units, 1, tokens), jnp.float32),
            pltpu.VMEM((units, 1, tokens), jnp.float32),
            pltpu.VMEM((units, head_dim, tokens), jnp.float32),
            pltpu.SemaphoreType.DMA((2 * capacity + 1,)),
            pltpu.SemaphoreType.DMA((slots,)),
            pltpu.SemaphoreType.DMA((32,)),
            pltpu.SemaphoreType.DMA((14,)),
            pltpu.SemaphoreType.DMA((14,)),
            pltpu.SemaphoreType.DMA((12,)),
        ],
        compiler_params=pltpu.CompilerParams(
            collective_id=0, has_side_effects=True, vmem_limit_bytes=48 * 1024 * 1024
        ),
        cost_estimate=pl.CostEstimate(
            flops=4 * capacity * slots * tokens * tokens * channels,
            bytes_accessed=4 * queries.size * 2,
            transcendentals=capacity * slots * HEADS * tokens * tokens,
        ),
        name="gathered_attention",
    )(counts, neighbors, queries, keys, values)


def per_device(queries, keys, values, counts, neighbors):
    if counts.shape[0] == LINE * 2 * CORES and queries.shape[1] == queries.shape[2] and queries.shape[0] == 4:
        return gathered_attention(queries, keys, values, counts, neighbors)
    return ring_attention(queries, keys, values, counts, neighbors)


def solution(mesh):
    in_specs = (
        P(("clip", "tile"), None, None),
        P(("clip", "tile"), None, None),
        P(("clip", "tile"), None, None),
        P("clip"),
        P("clip", None),
    )
    out_specs = P(("clip", "tile"), None, None)
    return jax.shard_map(
        per_device, mesh=mesh, in_specs=in_specs, out_specs=out_specs, check_vma=False
    )
```
